32 devices in a mesh: parts: 2 (over y), blk: 4 (over z), ao: 2 (over x), sub: 2 (over core).
Axes of the slice: x: 2, y: 2, z: 4, core: 2. Of those that a mesh axis runs over, the one named last changes fastest.
Arguments:
- coulomb_three: bfloat16 [1024, 256, 512], P(('parts', 'ao'), ('blk', 'sub')), parts along dimension 0, may hold values from -0.23925781 to 0.23925781
- three_mask: int32 [64, 16, 32], P(('parts', 'ao'), ('blk', 'sub')), parts along dimension 0, may hold values 0 or 1
- g_occ: bfloat16 [1024, 512], P(('parts', 'blk', 'sub')), parts along dimension 0, may hold values from -8 to 8
- g_virt: bfloat16 [1024, 512], P(('parts', 'blk', 'sub')), parts along dimension 0, may hold values from -8 to 8
- occ_mask: int32 [64, 32], P('parts'), parts along dimension 0, may hold values from 0 to 1, as said below
- virt_mask: int32 [64, 32], P('parts'), parts along dimension 0, may hold values from 0 to 1, as said below
Outputs:
- chi_band: float32 [512, 3, 32], P(('parts', 'blk', 'sub')), parts along dimension 0
The draws below stay inside these ranges and needn't reach their ends.
There are 2 independent parts, one for each index of `parts`. The reference program is written for one: setup_inputs(seed, part) draws one part's arguments, and reference() takes and returns one part's arrays. A program takes and returns all parts, laid end to end along the dimension named above; each array names one. Nothing has to cross between parts.
Inputs may be any that keep to these rules, and one draw needn't show every extreme that they name: `occ_mask`: symmetric; every diagonal block is 1. `virt_mask`: symmetric; every diagonal block is 1.
All inputs are finite; a program needn't handle non-finite values. No bound on the sum of `three_mask` on one device may be relied on, other than what follows from the above.
Results may differ from the reference program's by a relative error of at most 0.0003.
Values may be sent and summed in bfloat16 or wider, within the bound.
A program may use at most 256 MiB of HBM per device.

```python
import jax
import jax.numpy as jnp
from jax import lax

NAO = 512
BS = 16
ABLK = 16
AUX_DEV = 32
REACH = 1
NAUX = 256


def green_panel(key, rough, coupling):
    keys = jax.random.split(key, 1)
    index = jnp.arange(NAO)
    distance = jnp.abs(index[:, None] - index[None, :]).astype(jnp.float32)
    diagonal = jax.random.uniform(keys[0], (NAO,), jnp.float32, 0.8, 1.6)
    middle = coupling * 0.5 * (rough + rough.T) * jnp.exp(-distance / (0.5 * NAO))
    matrix = jnp.where(index[:, None] == index[None, :], diagonal[:, None] + jnp.zeros_like(middle), middle)
    return matrix.astype(jnp.bfloat16)


def draw_g_occ(key, part):
    key = jax.random.fold_in(key, 11)
    keys = jax.random.split(key, 3)
    rough = jax.random.normal(keys[0], (NAO, NAO), jnp.float32)
    return green_panel(keys[2], rough, 0.12)


def draw_g_virt(key, part):
    key = jax.random.fold_in(key, 12)
    keys = jax.random.split(key, 3)
    rough = jax.random.normal(keys[0], (NAO, NAO), jnp.float32)
    return green_panel(keys[2], rough, 0.1)


def block_pattern(key):
    count = NAO // BS
    keys = jax.random.split(key, 3)
    raw = jax.random.randint(keys[0], (count, count), 0, 2, jnp.int32)
    index = jnp.arange(count, dtype=jnp.int32)
    upper = (index[:, None] < index[None, :]).astype(jnp.int32)
    half_mask = raw * upper
    joined = half_mask + half_mask.T
    first = jax.random.randint(keys[1], (), 0, count, jnp.int32)
    step = jax.random.randint(keys[2], (), 1, count, jnp.int32)
    second = (first + step) % count
    hole = jnp.logical_or(jnp.logical_and(index[:, None] == first, index[None, :] == second), jnp.logical_and(index[:, None] == second, index[None, :] == first))
    joined = jnp.where(hole, jnp.zeros_like(joined), joined)
    identity = (index[:, None] == index[None, :]).astype(jnp.int32)
    return jnp.maximum(joined, identity)


def draw_occ_mask(key, part):
    key = jax.random.fold_in(key, 13)
    return block_pattern(key)


def draw_virt_mask(key, part):
    key = jax.random.fold_in(key, 14)
    return block_pattern(key)


def with_ends(drawn, stream_key, smallest, top_value):
    longest = drawn.shape.index(max(drawn.shape))
    spots = []
    for shift in (0, 1):
        where = [jax.random.randint(jax.random.fold_in(stream_key, axis), (), 0, length) for axis, length in enumerate(drawn.shape)]
        where[longest] = (where[longest] + shift) % drawn.shape[longest]
        spots.append(tuple(where))
    return drawn.at[spots[0]].set(smallest).at[spots[1]].set(top_value)


def block_scale(key, dims, shards, smallest, high):
    level, own = 1.0, jax.random.fold_in(key, 6)
    for position, shards_of in shards:
        heights = jnp.exp(jax.random.uniform(jax.random.fold_in(own, position), (shards_of,), jnp.float32, smallest / len(shards), high / len(shards)))
        level = level * jnp.repeat(heights, dims[position] // shards_of).reshape([-1 if axis == position else 1 for axis in range(len(dims))])
    return level


def centred(rng, dims, spread, limit, cuts=(), kind=jnp.bfloat16):
    loudness = block_scale(rng, dims, cuts, -0.22, 0.18) if cuts else 1.0
    array = jax.random.normal(rng, dims, jnp.float32) * spread * loudness
    return jnp.minimum(jnp.maximum(array, -limit), limit).astype(kind)


def setup_inputs(seed: int = 0, part: int = 0) -> dict:
    seeds = jax.random.split(jax.random.key(seed), 7)
    own_keys = jax.random.split(jax.random.fold_in(seeds[6], part), 7)
    coulomb_three = centred(own_keys[0], (NAO, NAUX, NAO), 0.04, 0.23925781, ((0, 2), (1, 8)))
    three_mask = with_ends((jax.random.randint(own_keys[1], (NAO // BS, NAUX // ABLK, NAO // BS), 0, 4) < 3).astype(jnp.int32), jax.random.fold_in(own_keys[1], 1), 0, 1)
    g_occ = draw_g_occ(jax.random.fold_in(jax.random.fold_in(seeds[6], part), 71), part)
    g_virt = draw_g_virt(jax.random.fold_in(jax.random.fold_in(seeds[6], part), 71), part)
    occ_mask = draw_occ_mask(jax.random.fold_in(jax.random.fold_in(seeds[6], part), 71), part)
    virt_mask = draw_virt_mask(jax.random.fold_in(jax.random.fold_in(seeds[6], part), 71), part)
    return dict(coulomb_three=coulomb_three, three_mask=three_mask, g_occ=g_occ, g_virt=g_virt, occ_mask=occ_mask, virt_mask=virt_mask)


def mask_green(green, blocks):
    nblocks = blocks.shape[0]
    shaped = green.reshape(nblocks, BS, nblocks, BS)
    return (shaped * blocks[:, None, :, None].astype(green.dtype)).reshape(green.shape)


def mask_three(three_blk, mask_blk):
    nu_blocks = mask_blk.shape[0]
    aux_blocks = mask_blk.shape[1]
    mu_blocks = mask_blk.shape[2]
    shaped = three_blk.reshape(nu_blocks, BS, aux_blocks, ABLK, mu_blocks, BS)
    weights = mask_blk[:, None, :, None, :, None].astype(three_blk.dtype)
    return (shaped * weights).reshape(three_blk.shape)


def reference(coulomb_three, three_mask, g_occ, g_virt, occ_mask, virt_mask):
    occ_eff = mask_green(g_occ, occ_mask)
    virt_eff = mask_green(g_virt, virt_mask)
    nblk = NAUX // AUX_DEV
    mask_width = AUX_DEV // ABLK

    def block_tensor(index):
        start = (index * AUX_DEV).astype(jnp.int32)
        mask_start = (index * mask_width).astype(jnp.int32)
        three_blk = lax.dynamic_slice_in_dim(coulomb_three, start, AUX_DEV, 1)
        mask_blk = lax.dynamic_slice_in_dim(three_mask, mask_start, mask_width, 1)
        return mask_three(three_blk, mask_blk)

    def one_block(index):
        own = block_tensor(index)
        left = jnp.dot(own.reshape(NAO * AUX_DEV, NAO), occ_eff, preferred_element_type=jnp.float32)
        left = left.astype(jnp.bfloat16).reshape(NAO, AUX_DEV * NAO)
        right = jnp.dot(virt_eff.T, left, preferred_element_type=jnp.float32)
        right = right.astype(jnp.bfloat16).reshape(NAO, AUX_DEV, NAO).astype(jnp.float32)
        band_tiles = []
        for offset in range(-REACH, REACH + 1):
            target = index + offset
            inside = jnp.logical_and(target >= 0, target < nblk)
            other = block_tensor(jnp.clip(target, 0, nblk - 1).astype(jnp.int32)).astype(jnp.float32)
            tile = lax.dot_general(right, other, (((0, 2), (0, 2)), ((), ())))
            band_tiles.append(jnp.where(inside, tile, jnp.zeros_like(tile)))
        return jnp.stack(band_tiles, axis=1)

    blocks = lax.map(one_block, jnp.arange(nblk, dtype=jnp.int32))
    return blocks.reshape(NAUX, 2 * REACH + 1, AUX_DEV)
```

```python
import jax
import jax.numpy as jnp
from jax import lax
from jax.experimental import pallas as pl
from jax.experimental.pallas import tpu as pltpu
from jax.sharding import PartitionSpec as P

BS = 16
ABLK = 16
CHUNK = 128
VMEM_LIMIT = 48 * 1024 * 1024


def shift(x, axis, by):
    count = lax.axis_size(axis)
    pairs = [(i, i + by) for i in range(count) if 0 <= i + by < count]
    return lax.ppermute(x, axis, pairs)


def spread(blocks, size):
    row = lax.broadcasted_iota(jnp.int32, (blocks, size), 0)
    col = lax.broadcasted_iota(jnp.int32, (blocks, size), 1)
    return (row == col // BS).astype(jnp.bfloat16)


def widen_last(mask, size):
    count = mask.shape[-1]
    flat = mask.astype(jnp.bfloat16).reshape(-1, count)
    wide = jnp.dot(flat, spread(count, size), preferred_element_type=jnp.float32)
    return wide.astype(jnp.bfloat16).reshape(mask.shape[:-1] + (size,))


def mask_green(green, blocks):
    count = blocks.shape[0]
    wide = widen_last(blocks, green.shape[1])
    shaped = green.reshape(count, green.shape[0] // count, green.shape[1])
    return (shaped * wide[:, None, :]).reshape(green.shape)


def mask_three(three, mask):
    wide = widen_last(mask, three.shape[2])
    shaped = three.reshape(mask.shape[0], BS, mask.shape[1], ABLK, three.shape[2])
    return (shaped * wide[:, None, :, None, :]).reshape(three.shape)


def transform_kernel(own_ref, oth_ref, occ_ref, virt_ref, send_ref, keep_ref, left_ref, right_ref):
    half, share, depth = own_ref.shape
    width = occ_ref.shape[1]
    full = 2 * half
    step = 64
    occ = occ_ref[...]
    for which, ref in enumerate((own_ref, oth_ref)):

        @pl.loop(0, half // step)
        def _(i, ref=ref, which=which):
            rows = ref[pl.ds(i * step, step)].reshape(step * share, depth)
            at = pl.multiple_of((which * half + i * step) * share, step * share)
            left_ref[pl.ds(at, step * share), :] = jnp.dot(
                rows, occ, preferred_element_type=jnp.float32
            )

    for p in range(0, share, 2):
        pair = [left_ref[pl.ds(p + k, full, stride=share), :].astype(jnp.bfloat16) for k in (0, 1)]
        out = lax.dot_general(
            virt_ref[...],
            jnp.concatenate(pair, axis=1),
            (((0,), (0,)), ((), ())),
            preferred_element_type=jnp.float32,
        )
        for k in (0, 1):
            right_ref[pl.ds(p + k, full, stride=share), :] = out[:, k * width : (k + 1) * width]
    for which, ref in enumerate((send_ref, keep_ref)):

        @pl.loop(0, half // step)
        def _(i, ref=ref, which=which):
            at = pl.multiple_of((which * half + i * step) * share, step * share)
            rows = right_ref[pl.ds(at, step * share), :].astype(jnp.bfloat16)
            ref[pl.ds(i * step, step)] = rows.reshape(step, share, width)


def transform(own, oth, occ, virt):
    half, share, depth = own.shape
    width = occ.shape[1]
    out = jax.ShapeDtypeStruct((half, share, width), jnp.bfloat16)
    vmem = pl.BlockSpec(memory_space=pltpu.VMEM)
    return pl.pallas_call(
        transform_kernel,
        out_shape=(out, out),
        in_specs=[vmem] * 4,
        out_specs=(vmem, vmem),
        scratch_shapes=[pltpu.VMEM((2 * half * share, width), jnp.float32)] * 2,
        compiler_params=pltpu.CompilerParams(vmem_limit_bytes=VMEM_LIMIT),
        cost_estimate=pl.CostEstimate(
            flops=4 * half * share * width * (depth + 2 * half) * 2,
            bytes_accessed=4 * half * share * depth + 4 * half * share * width,
            transcendentals=0,
        ),
        name="transform",
    )(own, oth, occ, virt)


def band_kernel(right_ref, before_ref, here_ref, after_ref, out_ref):
    count, share, width = right_ref.shape

    @pl.when(pl.program_id(0) == 0)
    def _():
        out_ref[...] = jnp.zeros_like(out_ref)

    total = jnp.zeros(out_ref.shape, jnp.float32)
    for s in range(0, count, 2):
        rights = jnp.concatenate([right_ref[s], right_ref[s + 1]], axis=1)
        threes = jnp.concatenate(
            [
                jnp.concatenate([ref[s], ref[s + 1]], axis=1)
                for ref in (before_ref, here_ref, after_ref)
            ],
            axis=0,
        )
        total += lax.dot_general(
            rights, threes, (((1,), (1,)), ((), ())), preferred_element_type=jnp.float32
        )
    out_ref[...] += total


def band(right, threes, chunk):
    half, share, width = right.shape
    aux = threes[0].shape[1]
    rows = 32
    block = pl.BlockSpec((rows, aux, width), lambda i: (i, 0, chunk))
    return pl.pallas_call(
        band_kernel,
        grid=(half // rows,),
        out_shape=jax.ShapeDtypeStruct((share, 3 * aux), jnp.float32),
        in_specs=[pl.BlockSpec((rows, share, width), lambda i: (i, 0, 0))] + [block] * 3,
        out_specs=pl.BlockSpec((share, 3 * aux), lambda i: (0, 0)),
        compiler_params=pltpu.CompilerParams(vmem_limit_bytes=VMEM_LIMIT),
        cost_estimate=pl.CostEstimate(
            flops=2 * half * share * 3 * aux * width * 8,
            bytes_accessed=2 * half * width * (share + 3 * aux),
            transcendentals=0,
        ),
        name="band",
    )(right, *threes)


def body_pair(three, three_mask, g_occ, g_virt, occ_mask, virt_mask):
    half, aux, depth = three.shape
    share = aux // 2
    me = lax.axis_index("ao")
    swap = [(0, 1), (1, 0)]
    eff = mask_three(three, three_mask)
    low, high = eff[:, :share], eff[:, share:]
    first = me == 0
    own = jnp.where(first, low, high)
    oth = lax.ppermute(jnp.where(first, high, low), "ao", swap)
    both = lax.all_gather(jnp.stack([g_occ, g_virt]), ("blk", "sub"), axis=1, tiled=True)
    occ = mask_green(both[0], occ_mask)
    virt = mask_green(both[1], virt_mask)
    rows = jnp.where(first, virt, jnp.concatenate([virt[half:], virt[:half]], axis=0))
    virt = jnp.where(first, jnp.concatenate([rows[:, half:], rows[:, :half]], axis=1), rows)
    threes = (shift(eff, ("blk", "sub"), 1), eff, shift(eff, ("blk", "sub"), -1))
    kept, got = 0.0, 0.0
    for c in range(depth // CHUNK):
        send, keep = transform(own, oth, occ[:, c * CHUNK : (c + 1) * CHUNK], virt)
        recv = lax.ppermute(send, "ao", swap)
        kept = kept + band(keep, threes, c)
        got = got + band(recv, threes, c)
    chi = jnp.where(
        first, jnp.concatenate([kept, got], axis=0), jnp.concatenate([got, kept], axis=0)
    )
    return lax.psum(chi, "ao").reshape(aux, 3, aux)


def body_any(three, three_mask, g_occ, g_virt, occ_mask, virt_mask):
    eff = mask_three(three, three_mask)
    occ = mask_green(lax.all_gather(g_occ, ("blk", "sub"), axis=0, tiled=True), occ_mask)
    virt = mask_green(lax.all_gather(g_virt, ("blk", "sub"), axis=0, tiled=True), virt_mask)
    whole = lax.all_to_all(eff, "ao", split_axis=1, concat_axis=0, tiled=True)
    left = lax.dot_general(
        whole, occ, (((2,), (0,)), ((), ())), preferred_element_type=jnp.float32
    ).astype(jnp.bfloat16)
    right = lax.dot_general(
        virt, left, (((0,), (0,)), ((), ())), preferred_element_type=jnp.float32
    ).astype(jnp.bfloat16)
    right = lax.all_to_all(right, "ao", split_axis=0, concat_axis=1, tiled=True)
    tiles = [
        lax.dot_general(
            right, other, (((0, 2), (0, 2)), ((), ())), preferred_element_type=jnp.float32
        )
        for other in (shift(eff, ("blk", "sub"), 1), eff, shift(eff, ("blk", "sub"), -1))
    ]
    return lax.psum(jnp.stack(tiles, axis=1), "ao")


def solution(mesh):
    placed = (
        P(("parts", "ao"), ("blk", "sub"), None),
        P(("parts", "ao"), ("blk", "sub"), None),
        P(("parts", "blk", "sub"), None),
        P(("parts", "blk", "sub"), None),
        P("parts", None),
        P("parts", None),
    )
    return jax.shard_map(
        body_pair if mesh.shape["ao"] == 2 else body_any,
        mesh=mesh,
        in_specs=placed,
        out_specs=P(("parts", "blk", "sub"), None, None),
        check_vma=False,
    )
```

```python
import functools

import jax
import jax.numpy as jnp
from jax import lax
from jax.experimental import pallas as pl
from jax.experimental.pallas import tpu as pltpu
from jax.sharding import PartitionSpec as P

BS = 16
ABLK = 16
CHUNK = 128


def shift(x, axis, by):
    count = lax.axis_size(axis)
    pairs = [(i, i + by) for i in range(count) if 0 <= i + by < count]
    return lax.ppermute(x, axis, pairs)


def spread(blocks, size):
    row = lax.broadcasted_iota(jnp.int32, (blocks, size), 0)
    col = lax.broadcasted_iota(jnp.int32, (blocks, size), 1)
    return (row == col // BS).astype(jnp.bfloat16)


def widen_last(mask, size):
    count = mask.shape[-1]
    flat = mask.astype(jnp.bfloat16).reshape(-1, count)
    wide = jnp.dot(flat, spread(count, size), preferred_element_type=jnp.float32)
    return wide.astype(jnp.bfloat16).reshape(mask.shape[:-1] + (size,))


def mask_green(green, blocks):
    count = blocks.shape[0]
    wide = widen_last(blocks, green.shape[1])
    shaped = green.reshape(count, green.shape[0] // count, green.shape[1])
    return (shaped * wide[:, None, :]).reshape(green.shape)


def mask_three(three, mask):
    wide = widen_last(mask, three.shape[2])
    shaped = three.reshape(mask.shape[0], BS, mask.shape[1], ABLK, three.shape[2])
    return (shaped * wide[:, None, :, None, :]).reshape(three.shape)


PARTS = 4


def front_kernel(
    three_ref, wide_ref, eff_ref, oth_ref, before_ref, after_ref, held, load_sem, store_sem,
    edge_sem, pair_send, pair_recv, up_send, up_recv, down_send, down_recv,
):
    half, aux, depth = held.shape
    share = aux // 2
    part = half // PARTS
    subs = lax.axis_size("sub")
    count = lax.axis_size("blk") * subs
    me = lax.axis_index("blk") * subs + lax.axis_index("sub")
    ao = lax.axis_index("ao")
    above = jnp.minimum(me + 1, count - 1)
    below = jnp.maximum(me - 1, 0)
    pair_id = {"ao": 1 - ao}
    above_id = {"blk": above // subs, "sub": above % subs}
    below_id = {"blk": below // subs, "sub": below % subs}
    has_above, has_below = me < count - 1, me > 0
    spans = [pl.ds(k * part, part) for k in range(PARTS)]

    loads = [
        pltpu.make_async_copy(three_ref.at[s], held.at[s], load_sem.at[k])
        for k, s in enumerate(spans)
    ]
    for copy in loads:
        copy.start()
    barrier = pltpu.get_barrier_semaphore()
    pl.semaphore_signal(barrier, inc=1, device_id=pair_id, device_id_type=pl.DeviceIdType.MESH)

    @pl.when(has_above)
    def _():
        pl.semaphore_signal(
            barrier, inc=1, device_id=above_id, device_id_type=pl.DeviceIdType.MESH
        )

    @pl.when(has_below)
    def _():
        pl.semaphore_signal(
            barrier, inc=1, device_id=below_id, device_id_type=pl.DeviceIdType.MESH
        )

    theirs = pl.ds(pl.multiple_of((1 - ao) * share, share), share)

    def remote(src, dst, send, recv, k, device):
        return pltpu.make_async_remote_copy(
            src_ref=src,
            dst_ref=dst,
            send_sem=send.at[k],
            recv_sem=recv.at[k],
            device_id=device,
            device_id_type=pl.DeviceIdType.MESH,
        )

    pairs = [
        remote(held.at[s, theirs], oth_ref.at[s], pair_send, pair_recv, k, pair_id)
        for k, s in enumerate(spans)
    ]
    ups = [
        remote(held.at[s], before_ref.at[s], up_send, up_recv, k, above_id)
        for k, s in enumerate(spans)
    ]
    downs = [
        remote(held.at[s], after_ref.at[s], down_send, down_recv, k, below_id)
        for k, s in enumerate(spans)
    ]
    stores = [
        pltpu.make_async_copy(held.at[s], eff_ref.at[s], store_sem.at[k])
        for k, s in enumerate(spans)
    ]
    for k in range(PARTS):
        loads[k].wait()

        @pl.loop(0, part // BS)
        def _(i, k=k):
            row = k * (part // BS) + i
            for j in range(aux // ABLK):
                mask = wide_ref[pl.ds(row * (aux // ABLK) + j, 1), :].astype(jnp.bfloat16)
                at = (pl.ds(row * BS, BS), pl.ds(j * ABLK, ABLK))
                held[at] = held[at] * mask[None]

        if k == 0:
            pl.semaphore_wait(
                barrier, 1 + has_above.astype(jnp.int32) + has_below.astype(jnp.int32)
            )
        pairs[k].start()

        @pl.when(has_above)
        def _(k=k):
            ups[k].start()

        @pl.when(has_below)
        def _(k=k):
            downs[k].start()

        stores[k].start()

    @pl.when(jnp.logical_not(has_below))
    def _():
        copy = pltpu.make_async_copy(held, before_ref, edge_sem.at[0])
        copy.start()
        copy.wait()

    @pl.when(jnp.logical_not(has_above))
    def _():
        copy = pltpu.make_async_copy(held, after_ref, edge_sem.at[1])
        copy.start()
        copy.wait()

    for k in range(PARTS):
        stores[k].wait()

        @pl.when(has_above)
        def _(k=k):
            ups[k].wait_send()
            downs[k].wait_recv()

        @pl.when(has_below)
        def _(k=k):
            downs[k].wait_send()
            ups[k].wait_recv()

        pairs[k].wait()


def front(three, wide):
    half, aux, depth = three.shape
    hbm = pl.BlockSpec(memory_space=pl.ANY)
    whole = jax.ShapeDtypeStruct(three.shape, three.dtype)
    part = jax.ShapeDtypeStruct((half, aux // 2, depth), three.dtype)
    return pl.pallas_call(
        front_kernel,
        out_shape=(whole, part, whole, whole),
        in_specs=[hbm, pl.BlockSpec(memory_space=pltpu.VMEM)],
        out_specs=(hbm,) * 4,
        scratch_shapes=[pltpu.VMEM(three.shape, three.dtype)]
        + [pltpu.SemaphoreType.DMA((PARTS,))] * 2
        + [pltpu.SemaphoreType.DMA((2,))]
        + [pltpu.SemaphoreType.DMA((PARTS,))] * 6,
        compiler_params=pltpu.CompilerParams(
            collective_id=0, has_side_effects=True, vmem_limit_bytes=16 * 1024 * 1024
        ),
        cost_estimate=pl.CostEstimate(
            flops=10**11, bytes_accessed=10 * half * aux * depth, transcendentals=0
        ),
        name="front",
    )(three, wide)


def transform_kernel(has_sum, last, *refs):
    pieces = refs[: len(refs) - 5 - has_sum - last]
    refs = refs[len(pieces) :]
    occ_ref, virt_ref, sum_ref = refs[0], refs[1], refs[2] if has_sum else None
    out_refs = refs[2 + has_sum : -2]
    left_ref, right_ref = refs[-2:]
    if not last:
        right_ref = out_refs[0]
    share, depth = pieces[0].shape[1:]
    width = occ_ref.shape[1]
    have, full = virt_ref.shape
    half = full // 2
    step = 64
    occ = occ_ref[...]
    base = 0
    for ref in pieces:

        @pl.loop(0, ref.shape[0] // step)
        def _(i, ref=ref, base=base):
            rows = ref[pl.ds(i * step, step)].reshape(step * share, depth)
            at = pl.multiple_of((base + i * step) * share, step * share)
            left_ref[pl.ds(at, step * share), :] = jnp.dot(
                rows, occ, preferred_element_type=jnp.float32
            )

        base += ref.shape[0]

    for p in range(0, share, 2):
        pair = [left_ref[pl.ds(p + k, have, stride=share), :].astype(jnp.bfloat16) for k in (0, 1)]
        out = lax.dot_general(
            virt_ref[...],
            jnp.concatenate(pair, axis=1),
            (((0,), (0,)), ((), ())),
            preferred_element_type=jnp.float32,
        )
        for k in (0, 1):
            right_ref[pl.ds(p + k, full, stride=share), :] = out[:, k * width : (k + 1) * width]
    if not last:
        return
    for which, ref in enumerate(out_refs):

        @pl.loop(0, half // step)
        def _(i, ref=ref, which=which):
            at = pl.multiple_of((which * half + i * step) * share, step * share)
            rows = right_ref[pl.ds(at, step * share), :]
            if has_sum:
                rows += sum_ref[pl.ds(at, step * share), :]
            ref[pl.ds(i * step, step)] = rows.astype(jnp.bfloat16).reshape(step, share, width)


def transform(pieces, occ, virt, before=None, last=True):
    have, full = virt.shape
    share, depth = pieces[0].shape[1:]
    width = occ.shape[1]
    if last:
        out = (jax.ShapeDtypeStruct((full // 2, share, width), jnp.bfloat16),) * 2
    else:
        out = (jax.ShapeDtypeStruct((full * share, width), jnp.float32),)
    vmem = pl.BlockSpec(memory_space=pltpu.VMEM)
    operands = (*pieces, occ, virt) + (() if before is None else (before,))
    return pl.pallas_call(
        functools.partial(transform_kernel, int(before is not None), int(last)),
        out_shape=out,
        in_specs=[vmem] * len(operands),
        out_specs=(vmem,) * len(out),
        scratch_shapes=[
            pltpu.VMEM((have * share, width), jnp.float32),
            pltpu.VMEM((full * share, width) if last else (8, width), jnp.float32),
        ],
        compiler_params=pltpu.CompilerParams(vmem_limit_bytes=32 * 1024 * 1024),
        cost_estimate=pl.CostEstimate(
            flops=10 * have * share * width * (depth + full),
            bytes_accessed=2 * have * share * depth + 4 * full * share * width,
            transcendentals=0,
        ),
        name="transform",
    )(*operands)


def band_kernel(right_ref, before_ref, here_ref, after_ref, out_ref):
    count, share, width = right_ref.shape

    @pl.when(pl.program_id(0) == 0)
    def _():
        out_ref[...] = jnp.zeros_like(out_ref)

    total = jnp.zeros(out_ref.shape, jnp.float32)
    for s in range(0, count, 2):
        rights = jnp.concatenate([right_ref[s], right_ref[s + 1]], axis=1)
        threes = jnp.concatenate(
            [
                jnp.concatenate([ref[s], ref[s + 1]], axis=1)
                for ref in (before_ref, here_ref, after_ref)
            ],
            axis=0,
        )
        total += lax.dot_general(
            rights, threes, (((1,), (1,)), ((), ())), preferred_element_type=jnp.float32
        )
    out_ref[...] += total


def band(right, threes, chunk, start=0):
    half, share, width = right.shape
    aux = threes[0].shape[1]
    rows = 32
    block = pl.BlockSpec((rows, aux, width), lambda i: (i + start // rows, 0, chunk))
    return pl.pallas_call(
        band_kernel,
        grid=(half // rows,),
        out_shape=jax.ShapeDtypeStruct((share, 3 * aux), jnp.float32),
        in_specs=[pl.BlockSpec((rows, share, width), lambda i: (i, 0, 0))] + [block] * 3,
        out_specs=pl.BlockSpec((share, 3 * aux), lambda i: (0, 0)),
        compiler_params=pltpu.CompilerParams(vmem_limit_bytes=16 * 1024 * 1024),
        cost_estimate=pl.CostEstimate(
            flops=2 * half * share * 3 * aux * width * 64,
            bytes_accessed=2 * half * width * (share + 3 * aux),
            transcendentals=0,
        ),
        name="band",
    )(right, *threes)


def body_pair(three, three_mask, g_occ, g_virt, occ_mask, virt_mask):
    half, aux, depth = three.shape
    share = aux // 2
    me = lax.axis_index("ao")
    swap = [(0, 1), (1, 0)]
    first = me == 0
    both = lax.all_gather(jnp.stack([g_occ, g_virt]), ("blk", "sub"), axis=1, tiled=True)
    wide = widen_last(three_mask, depth).reshape(-1, depth).astype(jnp.float32)
    eff, oth, before, after = front(three, wide)
    threes = (before, eff, after)
    own = jnp.where(first, eff[:, :share], eff[:, share:])
    occ = mask_green(both[0], occ_mask)
    virt = mask_green(both[1], virt_mask)
    virt = jnp.where(first, virt, jnp.concatenate([virt[half:], virt[:half]], axis=0))
    virt = jnp.where(first, jnp.concatenate([virt[:, half:], virt[:, :half]], axis=1), virt)
    kept, returned = 0.0, []
    chunks = depth // CHUNK
    for c in range(chunks):
        occ_c = occ[:, c * CHUNK : (c + 1) * CHUNK]
        send, keep = transform((own, oth), occ_c, virt)
        send, own, virt = lax.optimization_barrier((send, own, virt))
        cuts = (0, half) if c < chunks - 1 else (0, half // 2, half)
        for start, stop in zip(cuts, cuts[1:]):
            returned.append((lax.ppermute(send[start:stop], "ao", swap), c, start))
        kept = kept + band(keep, threes, c)
    got = 0.0
    for recv, c, start in returned:
        if c == chunks - 1:
            recv, kept = lax.optimization_barrier((recv, kept))
        got = got + band(recv, threes, c, start)
    chi = jnp.where(
        first, jnp.concatenate([kept, got], axis=0), jnp.concatenate([got, kept], axis=0)
    )
    chi = chi + lax.ppermute(chi, "ao", swap)
    tiles = chi.reshape(aux, 3, aux)
    index = lax.axis_index(("blk", "sub"))
    offset = index - 1 + lax.broadcasted_iota(jnp.int32, tiles.shape, 1)
    inside = jnp.logical_and(offset >= 0, offset < lax.axis_size(("blk", "sub")))
    return jnp.where(inside, tiles, 0.0)


def body_any(three, three_mask, g_occ, g_virt, occ_mask, virt_mask):
    eff = mask_three(three, three_mask)
    occ = mask_green(lax.all_gather(g_occ, ("blk", "sub"), axis=0, tiled=True), occ_mask)
    virt = mask_green(lax.all_gather(g_virt, ("blk", "sub"), axis=0, tiled=True), virt_mask)
    whole = lax.all_to_all(eff, "ao", split_axis=1, concat_axis=0, tiled=True)
    left = lax.dot_general(
        whole, occ, (((2,), (0,)), ((), ())), preferred_element_type=jnp.float32
    ).astype(jnp.bfloat16)
    right = lax.dot_general(
        virt, left, (((0,), (0,)), ((), ())), preferred_element_type=jnp.float32
    ).astype(jnp.bfloat16)
    right = lax.all_to_all(right, "ao", split_axis=0, concat_axis=1, tiled=True)
    tiles = [
        lax.dot_general(
            right, other, (((0, 2), (0, 2)), ((), ())), preferred_element_type=jnp.float32
        )
        for other in (shift(eff, ("blk", "sub"), 1), eff, shift(eff, ("blk", "sub"), -1))
    ]
    return lax.psum(jnp.stack(tiles, axis=1), "ao")


def solution(mesh):
    placed = (
        P(("parts", "ao"), ("blk", "sub"), None),
        P(("parts", "ao"), ("blk", "sub"), None),
        P(("parts", "blk", "sub"), None),
        P(("parts", "blk", "sub"), None),
        P("parts", None),
        P("parts", None),
    )
    return jax.shard_map(
        body_pair if mesh.shape["ao"] == 2 else body_any,
        mesh=mesh,
        in_specs=placed,
        out_specs=P(("parts", "blk", "sub"), None, None),
        check_vma=False,
    )
```

```python
import jax
import jax.numpy as jnp
from jax import lax
from jax.experimental import pallas as pl
from jax.experimental.pallas import tpu as pltpu
from jax.sharding import PartitionSpec as P

BS = 16
ABLK = 16
CHUNK = 128


def shift(x, axis, by):
    count = lax.axis_size(axis)
    pairs = [(i, i + by) for i in range(count) if 0 <= i + by < count]
    return lax.ppermute(x, axis, pairs)


def spread(blocks, size):
    row = lax.broadcasted_iota(jnp.int32, (blocks, size), 0)
    col = lax.broadcasted_iota(jnp.int32, (blocks, size), 1)
    return (row == col // BS).astype(jnp.bfloat16)


def widen_last(mask, size):
    count = mask.shape[-1]
    flat = mask.astype(jnp.bfloat16).reshape(-1, count)
    wide = jnp.dot(flat, spread(count, size), preferred_element_type=jnp.float32)
    return wide.astype(jnp.bfloat16).reshape(mask.shape[:-1] + (size,))


def mask_green(green, blocks):
    count = blocks.shape[0]
    wide = widen_last(blocks, green.shape[1])
    shaped = green.reshape(count, green.shape[0] // count, green.shape[1])
    return (shaped * wide[:, None, :]).reshape(green.shape)


def mask_three(three, mask):
    wide = widen_last(mask, three.shape[2])
    shaped = three.reshape(mask.shape[0], BS, mask.shape[1], ABLK, three.shape[2])
    return (shaped * wide[:, None, :, None, :]).reshape(three.shape)


PARTS = 4
STEP = 64
MESH = pl.DeviceIdType.MESH


def pair_kernel(
    three_ref, wide_ref, occ_in, virt_in, occ_wide, virt_wide, out_ref,
    held, oth, before, after, green, left, right, send, keep, recv, mine, extra,
    load_sem, green_send, green_recv, pair_send, pair_recv, up_send, up_recv,
    down_send, down_recv, back_send, back_recv, sum_sem,
):
    half, aux, depth = held.shape
    share = aux // 2
    full = 2 * half
    part = half // PARTS
    rows_g = occ_in.shape[0]
    subs = lax.axis_size("sub")
    count = lax.axis_size("blk") * subs
    me = lax.axis_index("blk") * subs + lax.axis_index("sub")
    ao = lax.axis_index("ao")
    pair_id = {"ao": 1 - ao}
    has_above, has_below = me < count - 1, me > 0

    def at_index(index):
        return {"blk": index // subs, "sub": index % subs}

    above_id = at_index(jnp.minimum(me + 1, count - 1))
    below_id = at_index(jnp.maximum(me - 1, 0))
    peers = [at_index(lax.rem(me + d, count)) for d in range(1, count)]
    spans = [pl.ds(k * part, part) for k in range(PARTS)]
    loads = [
        pltpu.make_async_copy(three_ref.at[s], held.at[s], load_sem.at[k])
        for k, s in enumerate(spans)
    ]
    for copy in loads:
        copy.start()
    barrier = pltpu.get_barrier_semaphore()
    for device in [pair_id] + peers:
        pl.semaphore_signal(barrier, inc=1, device_id=device, device_id_type=MESH)

    own_rows = pl.ds(pl.multiple_of(me * rows_g, rows_g), rows_g)
    green[0, own_rows] = occ_in[...]
    green[1, own_rows] = virt_in[...]

    def remote(src, dst, send_sem, recv_sem, device):
        return pltpu.make_async_remote_copy(
            src_ref=src, dst_ref=dst, send_sem=send_sem, recv_sem=recv_sem,
            device_id=device, device_id_type=MESH,
        )

    ours = pl.ds(pl.multiple_of(ao * share, share), share)
    theirs = pl.ds(pl.multiple_of((1 - ao) * share, share), share)
    greens = [
        remote(green.at[g, own_rows], green.at[g, own_rows],
               green_send.at[g, d], green_recv.at[g, d], peers[d])
        for g in (0, 1) for d in range(count - 1)
    ]
    pairs = [
        remote(held.at[s, theirs], oth.at[s], pair_send.at[k], pair_recv.at[k], pair_id)
        for k, s in enumerate(spans)
    ]
    ups = [
        remote(held.at[s], before.at[s], up_send.at[k], up_recv.at[k], above_id)
        for k, s in enumerate(spans)
    ]
    downs = [
        remote(held.at[s], after.at[s], down_send.at[k], down_recv.at[k], below_id)
        for k, s in enumerate(spans)
    ]
    for k in range(PARTS):
        loads[k].wait()

        @pl.loop(0, part // BS)
        def _(i, k=k):
            row = k * (part // BS) + i
            for j in range(aux // ABLK):
                mask = wide_ref[pl.ds(row * (aux // ABLK) + j, 1), :].astype(jnp.bfloat16)
                at = (pl.ds(row * BS, BS), pl.ds(j * ABLK, ABLK))
                held[at] = held[at] * mask[None]

        if k == 0:
            pl.semaphore_wait(barrier, count)
        pairs[k].start()
        if k == 0:
            for copy in greens:
                copy.start()

        @pl.when(has_above)
        def _(k=k):
            ups[k].start()

        @pl.when(has_below)
        def _(k=k):
            downs[k].start()

    @pl.when(jnp.logical_not(has_below))
    def _():
        @pl.loop(0, half)
        def _(i):
            before[i] = jnp.zeros((aux, depth), jnp.bfloat16)

    @pl.when(jnp.logical_not(has_above))
    def _():
        @pl.loop(0, half)
        def _(i):
            after[i] = jnp.zeros((aux, depth), jnp.bfloat16)

    for copy in greens:
        copy.wait()
    for g, wide in ((0, occ_wide), (1, virt_wide)):

        @pl.loop(0, full // BS)
        def _(i, g=g, wide=wide):
            at = pl.ds(i * BS, BS)
            green[g, at] = green[g, at] * wide[pl.ds(i, 1), :].astype(jnp.bfloat16)

    def to_left(source, start, stop, first_n, c):
        lanes = pl.ds(c * CHUNK, CHUNK)

        @pl.loop(start // STEP, stop // STEP)
        def _(i):
            rows = source(i * STEP).reshape(STEP * share, depth)
            at = pl.multiple_of((first_n + i * STEP) * share, STEP * share)
            left[pl.ds(at, STEP * share), :] = jnp.dot(
                rows, green[0, :, lanes], preferred_element_type=jnp.float32
            )

    def of_own(n):
        return held[pl.ds(n, STEP), ours]

    def of_oth(n):
        return oth[pl.ds(n, STEP)]

    def to_right(c):
        for p in range(0, share, 2):
            both = [left[pl.ds(p + k, full, stride=share), :].astype(jnp.bfloat16) for k in (0, 1)]
            out = lax.dot_general(
                green[1],
                jnp.concatenate(both, axis=1),
                (((0,), (0,)), ((), ())),
                preferred_element_type=jnp.float32,
            )
            for k in (0, 1):
                right[pl.ds(p + k, full, stride=share), :] = out[:, k * CHUNK : (k + 1) * CHUNK]

    def out_of_right(ref, c, first_s):
        @pl.loop(0, half // STEP)
        def _(i):
            at = pl.multiple_of((first_s + i * STEP) * share, STEP * share)
            rows = right[pl.ds(at, STEP * share), :].astype(jnp.bfloat16)
            ref[c, pl.ds(i * STEP, STEP)] = rows.reshape(STEP, share, CHUNK)

    def band(ref, c, start, stop):
        lanes = pl.ds(c * CHUNK, CHUNK)

        def some(i, total):
            for k in range(0, 16, 2):
                s = i * 16 + k
                rights = jnp.concatenate([ref[c, s], ref[c, s + 1]], axis=1)
                threes = [
                    jnp.concatenate([t[s, :, lanes], t[s + 1, :, lanes]], axis=1)
                    for t in (before, held, after)
                ]
                total += lax.dot_general(
                    rights, jnp.concatenate(threes, axis=0), (((1,), (1,)), ((), ())),
                    preferred_element_type=jnp.float32,
                )
            return total

        zero = jnp.zeros((share, 3 * aux), jnp.float32)
        return lax.fori_loop(start // 16, stop // 16, some, zero)

    chunks = depth // CHUNK
    cuts = [(c, 0, half) for c in range(chunks - 1)]
    cuts += [(chunks - 1, 0, half // 2), (chunks - 1, half // 2, half)]
    backs = [
        remote(send.at[c, pl.ds(start, stop - start)], recv.at[c, pl.ds(start, stop - start)],
               back_send.at[k], back_recv.at[k], pair_id)
        for k, (c, start, stop) in enumerate(cuts)
    ]
    own_n, oth_n = ao * half, (1 - ao) * half
    for c in range(chunks):
        to_left(of_own, 0, half, own_n, c)
        for k in range(PARTS):
            if c == 0:
                pairs[k].wait()
            to_left(of_oth, k * part, (k + 1) * part, oth_n, c)
        to_right(c)
        out_of_right(send, c, oth_n)
        for k, cut in enumerate(cuts):
            if cut[0] == c:
                backs[k].start()
        out_of_right(keep, c, own_n)

    for k in range(PARTS):

        @pl.when(has_above)
        def _(k=k):
            ups[k].wait_send()
            downs[k].wait_recv()

        @pl.when(has_below)
        def _(k=k):
            downs[k].wait_send()
            ups[k].wait_recv()

    total = band(keep, 0, 0, half)
    for c in range(1, chunks):
        total += band(keep, c, 0, half)
    mine[ours] = total
    total = jnp.zeros((share, 3 * aux), jnp.float32)
    for k, (c, start, stop) in enumerate(cuts):
        backs[k].wait()
        total += band(recv, c, start, stop)
    mine[theirs] = total
    last = remote(mine, extra, sum_sem.at[0], sum_sem.at[1], pair_id)
    last.start()
    last.wait()
    out_ref[...] = mine[...] + extra[...]


def pair_call(three, wide, g_occ, g_virt, occ_wide, virt_wide, peers):
    half, aux, depth = three.shape
    share = aux // 2
    vmem = pl.BlockSpec(memory_space=pltpu.VMEM)
    part = (half, share, depth)
    back = (depth // CHUNK, half, share, CHUNK)
    dma = pltpu.SemaphoreType.DMA
    backs = depth // CHUNK + 1
    return pl.pallas_call(
        pair_kernel,
        out_shape=jax.ShapeDtypeStruct((aux, 3 * aux), jnp.float32),
        in_specs=[pl.BlockSpec(memory_space=pl.ANY)] + [vmem] * 5,
        out_specs=vmem,
        scratch_shapes=[
            pltpu.VMEM(three.shape, three.dtype),
            pltpu.VMEM(part, three.dtype),
            pltpu.VMEM(three.shape, three.dtype),
            pltpu.VMEM(three.shape, three.dtype),
            pltpu.VMEM((2, depth, depth), three.dtype),
            pltpu.VMEM((2 * half * share, CHUNK), jnp.float32),
            pltpu.VMEM((2 * half * share, CHUNK), jnp.float32),
            pltpu.VMEM(back, three.dtype),
            pltpu.VMEM(back, three.dtype),
            pltpu.VMEM(back, three.dtype),
            pltpu.VMEM((aux, 3 * aux), jnp.float32),
            pltpu.VMEM((aux, 3 * aux), jnp.float32),
            dma((PARTS,)),
            dma((2, peers)),
            dma((2, peers)),
        ]
        + [dma((PARTS,))] * 6
        + [dma((backs,))] * 2
        + [dma((2,))],
        compiler_params=pltpu.CompilerParams(
            collective_id=0, has_side_effects=True, vmem_limit_bytes=58 * 1024 * 1024
        ),
        cost_estimate=pl.CostEstimate(
            flops=10**11, bytes_accessed=2 * half * aux * depth, transcendentals=0
        ),
        name="pair",
    )(three, wide, g_occ, g_virt, occ_wide, virt_wide)


def body_pair(three, three_mask, g_occ, g_virt, occ_mask, virt_mask):
    half, aux, depth = three.shape
    masks = jnp.concatenate([three_mask.reshape(-1, depth // BS), occ_mask, virt_mask], axis=0)
    wide = widen_last(masks, depth).astype(jnp.float32)
    count = three_mask.shape[0] * three_mask.shape[1]
    blocks = occ_mask.shape[0]
    peers = lax.axis_size(("blk", "sub")) - 1
    chi = pair_call(
        three, wide[:count], g_occ, g_virt,
        wide[count : count + blocks], wide[count + blocks :], peers,
    )
    return chi.reshape(aux, 3, aux)


def body_any(three, three_mask, g_occ, g_virt, occ_mask, virt_mask):
    eff = mask_three(three, three_mask)
    occ = mask_green(lax.all_gather(g_occ, ("blk", "sub"), axis=0, tiled=True), occ_mask)
    virt = mask_green(lax.all_gather(g_virt, ("blk", "sub"), axis=0, tiled=True), virt_mask)
    whole = lax.all_to_all(eff, "ao", split_axis=1, concat_axis=0, tiled=True)
    left = lax.dot_general(
        whole, occ, (((2,), (0,)), ((), ())), preferred_element_type=jnp.float32
    ).astype(jnp.bfloat16)
    right = lax.dot_general(
        virt, left, (((0,), (0,)), ((), ())), preferred_element_type=jnp.float32
    ).astype(jnp.bfloat16)
    right = lax.all_to_all(right, "ao", split_axis=0, concat_axis=1, tiled=True)
    tiles = [
        lax.dot_general(
            right, other, (((0, 2), (0, 2)), ((), ())), preferred_element_type=jnp.float32
        )
        for other in (shift(eff, ("blk", "sub"), 1), eff, shift(eff, ("blk", "sub"), -1))
    ]
    return lax.psum(jnp.stack(tiles, axis=1), "ao")


def solution(mesh):
    placed = (
        P(("parts", "ao"), ("blk", "sub"), None),
        P(("parts", "ao"), ("blk", "sub"), None),
        P(("parts", "blk", "sub"), None),
        P(("parts", "blk", "sub"), None),
        P("parts", None),
        P("parts", None),
    )
    return jax.shard_map(
        body_pair if mesh.shape["ao"] == 2 else body_any,
        mesh=mesh,
        in_specs=placed,
        out_specs=P(("parts", "blk", "sub"), None, None),
        check_vma=False,
    )
```

```python
import jax
import jax.numpy as jnp
from jax import lax
from jax.experimental import pallas as pl
from jax.experimental.pallas import tpu as pltpu
from jax.sharding import PartitionSpec as P

BS = 16
ABLK = 16
CHUNK = 128


def shift(x, axis, by):
    count = lax.axis_size(axis)
    pairs = [(i, i + by) for i in range(count) if 0 <= i + by < count]
    return lax.ppermute(x, axis, pairs)


def spread(blocks, size):
    row = lax.broadcasted_iota(jnp.int32, (blocks, size), 0)
    col = lax.broadcasted_iota(jnp.int32, (blocks, size), 1)
    return (row == col // BS).astype(jnp.bfloat16)


def widen_last(mask, size):
    count = mask.shape[-1]
    flat = mask.astype(jnp.bfloat16).reshape(-1, count)
    wide = jnp.dot(flat, spread(count, size), preferred_element_type=jnp.float32)
    return wide.astype(jnp.bfloat16).reshape(mask.shape[:-1] + (size,))


def mask_green(green, blocks):
    count = blocks.shape[0]
    wide = widen_last(blocks, green.shape[1])
    shaped = green.reshape(count, green.shape[0] // count, green.shape[1])
    return (shaped * wide[:, None, :]).reshape(green.shape)


def mask_three(three, mask):
    wide = widen_last(mask, three.shape[2])
    shaped = three.reshape(mask.shape[0], BS, mask.shape[1], ABLK, three.shape[2])
    return (shaped * wide[:, None, :, None, :]).reshape(three.shape)


PARTS = 4
STEP = 64
MESH = pl.DeviceIdType.MESH


def pair_kernel(
    three_ref, mask_ref, occ_in, virt_in, occ_mask, virt_mask, out_ref,
    held, oth, before, after, green, left, right, send, keep, recv, mine, extra,
    wide_ref, occ_wide, virt_wide,
    load_sem, green_send, green_recv, pair_send, pair_recv, up_send, up_recv,
    down_send, down_recv, back_send, back_recv, sum_sem,
):
    half, aux, depth = held.shape
    share = aux // 2
    full = 2 * half
    part = half // PARTS
    rows_g = occ_in.shape[0]
    subs = lax.axis_size("sub")
    count = lax.axis_size("blk") * subs
    me = lax.axis_index("blk") * subs + lax.axis_index("sub")
    ao = lax.axis_index("ao")
    pair_id = {"ao": 1 - ao}
    has_above, has_below = me < count - 1, me > 0

    def at_index(index):
        return {"blk": index // subs, "sub": index % subs}

    above_id = at_index(jnp.minimum(me + 1, count - 1))
    below_id = at_index(jnp.maximum(me - 1, 0))
    peers = [at_index(lax.rem(me + d, count)) for d in range(1, count)]
    spans = [pl.ds(k * part, part) for k in range(PARTS)]
    loads = [
        pltpu.make_async_copy(three_ref.at[s], held.at[s], load_sem.at[k])
        for k, s in enumerate(spans)
    ]
    for copy in loads:
        copy.start()
    barrier = pltpu.get_barrier_semaphore()
    for device in [pair_id] + peers:
        pl.semaphore_signal(barrier, inc=1, device_id=device, device_id_type=MESH)

    def widen(mask):
        spreading = spread(mask.shape[1], depth)
        flat = mask.astype(jnp.float32).astype(jnp.bfloat16)
        return jnp.dot(flat, spreading, preferred_element_type=jnp.float32)

    wide_ref[...] = widen(mask_ref[...])
    own_rows = pl.ds(pl.multiple_of(me * rows_g, rows_g), rows_g)
    green[0, own_rows] = occ_in[...]
    green[1, own_rows] = virt_in[...]

    def remote(src, dst, send_sem, recv_sem, device):
        return pltpu.make_async_remote_copy(
            src_ref=src, dst_ref=dst, send_sem=send_sem, recv_sem=recv_sem,
            device_id=device, device_id_type=MESH,
        )

    ours = pl.ds(pl.multiple_of(ao * share, share), share)
    theirs = pl.ds(pl.multiple_of((1 - ao) * share, share), share)
    greens = [
        remote(green.at[g, own_rows], green.at[g, own_rows],
               green_send.at[g, d], green_recv.at[g, d], peers[d])
        for g in (0, 1) for d in range(count - 1)
    ]
    pairs = [
        remote(held.at[s, theirs], oth.at[s], pair_send.at[k], pair_recv.at[k], pair_id)
        for k, s in enumerate(spans)
    ]
    ups = [
        remote(held.at[s], before.at[s], up_send.at[k], up_recv.at[k], above_id)
        for k, s in enumerate(spans)
    ]
    downs = [
        remote(held.at[s], after.at[s], down_send.at[k], down_recv.at[k], below_id)
        for k, s in enumerate(spans)
    ]
    for k in range(PARTS):
        loads[k].wait()

        @pl.loop(0, part // BS)
        def _(i, k=k):
            row = k * (part // BS) + i
            for j in range(aux // ABLK):
                mask = wide_ref[pl.ds(row * (aux // ABLK) + j, 1), :].astype(jnp.bfloat16)
                at = (pl.ds(row * BS, BS), pl.ds(j * ABLK, ABLK))
                held[at] = held[at] * mask[None]

        if k == 0:
            pl.semaphore_wait(barrier, count)
        pairs[k].start()
        if k == 0:
            for copy in greens:
                copy.start()

        @pl.when(has_above)
        def _(k=k):
            ups[k].start()

        @pl.when(has_below)
        def _(k=k):
            downs[k].start()

    @pl.when(jnp.logical_not(has_below))
    def _():
        @pl.loop(0, half)
        def _(i):
            before[i] = jnp.zeros((aux, depth), jnp.bfloat16)

    @pl.when(jnp.logical_not(has_above))
    def _():
        @pl.loop(0, half)
        def _(i):
            after[i] = jnp.zeros((aux, depth), jnp.bfloat16)

    for copy in greens:
        copy.wait()
    occ_wide[...] = widen(occ_mask[...])
    virt_wide[...] = widen(virt_mask[...])
    for g, wide in ((0, occ_wide), (1, virt_wide)):

        @pl.loop(0, full // BS)
        def _(i, g=g, wide=wide):
            at = pl.ds(i * BS, BS)
            green[g, at] = green[g, at] * wide[pl.ds(i, 1), :].astype(jnp.bfloat16)

    def to_left(source, start, stop, first_n, c):
        lanes = pl.ds(c * CHUNK, CHUNK)

        @pl.loop(start // STEP, stop // STEP)
        def _(i):
            rows = source(i * STEP).reshape(STEP * share, depth)
            at = pl.multiple_of((first_n + i * STEP) * share, STEP * share)
            left[pl.ds(at, STEP * share), :] = jnp.dot(
                rows, green[0, :, lanes], preferred_element_type=jnp.float32
            )

    def of_own(n):
        return held[pl.ds(n, STEP), ours]

    def of_oth(n):
        return oth[pl.ds(n, STEP)]

    def to_right(first_n, have, add):
        for p in range(0, share, 2):
            both = [left[pl.ds(first_n * share + p + k, have, stride=share), :] for k in (0, 1)]
            both = [x.astype(jnp.bfloat16) for x in both]
            out = lax.dot_general(
                green[1, pl.ds(first_n, have)],
                jnp.concatenate(both, axis=1),
                (((0,), (0,)), ((), ())),
                preferred_element_type=jnp.float32,
            )
            for k in (0, 1):
                rows = pl.ds(p + k, full, stride=share)
                term = out[:, k * CHUNK : (k + 1) * CHUNK]
                right[rows, :] = right[rows, :] + term if add else term

    def out_of_right(ref, c, first_s):
        @pl.loop(0, half // STEP)
        def _(i):
            at = pl.multiple_of((first_s + i * STEP) * share, STEP * share)
            rows = right[pl.ds(at, STEP * share), :].astype(jnp.bfloat16)
            ref[c, pl.ds(i * STEP, STEP)] = rows.reshape(STEP, share, CHUNK)

    def band(ref, c, start, stop):
        lanes = pl.ds(c * CHUNK, CHUNK)

        def some(i, total):
            for k in range(0, 16, 2):
                s = i * 16 + k
                rights = jnp.concatenate([ref[c, s], ref[c, s + 1]], axis=1)
                threes = [
                    jnp.concatenate([t[s, :, lanes], t[s + 1, :, lanes]], axis=1)
                    for t in (before, held, after)
                ]
                total += lax.dot_general(
                    rights, jnp.concatenate(threes, axis=0), (((1,), (1,)), ((), ())),
                    preferred_element_type=jnp.float32,
                )
            return total

        zero = jnp.zeros((share, 3 * aux), jnp.float32)
        return lax.fori_loop(start // 16, stop // 16, some, zero)

    chunks = depth // CHUNK
    cuts = [(c, 0, half) for c in range(chunks - 1)]
    cuts += [(chunks - 1, 0, half // 2), (chunks - 1, half // 2, half)]
    backs = [
        remote(send.at[c, pl.ds(start, stop - start)], recv.at[c, pl.ds(start, stop - start)],
               back_send.at[k], back_recv.at[k], pair_id)
        for k, (c, start, stop) in enumerate(cuts)
    ]
    own_n = pl.multiple_of(ao * half, half)
    oth_n = pl.multiple_of((1 - ao) * half, half)
    for c in range(chunks):
        to_left(of_own, 0, half, own_n, c)
        if c == 0:
            to_right(own_n, half, False)
        for k in range(PARTS):
            if c == 0:
                pairs[k].wait()
            to_left(of_oth, k * part, (k + 1) * part, oth_n, c)
        if c == 0:
            to_right(oth_n, half, True)
        else:
            to_right(0, full, False)
        out_of_right(send, c, oth_n)
        for k, cut in enumerate(cuts):
            if cut[0] == c:
                backs[k].start()
        out_of_right(keep, c, own_n)

    for k in range(PARTS):

        @pl.when(has_above)
        def _(k=k):
            ups[k].wait_send()
            downs[k].wait_recv()

        @pl.when(has_below)
        def _(k=k):
            downs[k].wait_send()
            ups[k].wait_recv()

    total = band(keep, 0, 0, half)
    for c in range(1, chunks):
        total += band(keep, c, 0, half)
    mine[ours] = total
    total = jnp.zeros((share, 3 * aux), jnp.float32)
    for k, (c, start, stop) in enumerate(cuts):
        backs[k].wait()
        total += band(recv, c, start, stop)
    mine[theirs] = total
    last = remote(mine, extra, sum_sem.at[0], sum_sem.at[1], pair_id)
    last.start()
    last.wait()
    out_ref[...] = mine[...] + extra[...]


def pair_call(three, mask, g_occ, g_virt, occ_mask, virt_mask, peers):
    half, aux, depth = three.shape
    share = aux // 2
    vmem = pl.BlockSpec(memory_space=pltpu.VMEM)
    part = (half, share, depth)
    back = (depth // CHUNK, half, share, CHUNK)
    dma = pltpu.SemaphoreType.DMA
    backs = depth // CHUNK + 1
    return pl.pallas_call(
        pair_kernel,
        out_shape=jax.ShapeDtypeStruct((aux, 3 * aux), jnp.float32),
        in_specs=[pl.BlockSpec(memory_space=pl.ANY)] + [vmem] * 5,
        out_specs=vmem,
        scratch_shapes=[
            pltpu.VMEM(three.shape, three.dtype),
            pltpu.VMEM(part, three.dtype),
            pltpu.VMEM(three.shape, three.dtype),
            pltpu.VMEM(three.shape, three.dtype),
            pltpu.VMEM((2, depth, depth), three.dtype),
            pltpu.VMEM((2 * half * share, CHUNK), jnp.float32),
            pltpu.VMEM((2 * half * share, CHUNK), jnp.float32),
            pltpu.VMEM(back, three.dtype),
            pltpu.VMEM(back, three.dtype),
            pltpu.VMEM(back, three.dtype),
            pltpu.VMEM((aux, 3 * aux), jnp.float32),
            pltpu.VMEM((aux, 3 * aux), jnp.float32),
            pltpu.VMEM((mask.shape[0], depth), jnp.float32),
            pltpu.VMEM((occ_mask.shape[0], depth), jnp.float32),
            pltpu.VMEM((virt_mask.shape[0], depth), jnp.float32),
            dma((PARTS,)),
            dma((2, peers)),
            dma((2, peers)),
        ]
        + [dma((PARTS,))] * 6
        + [dma((backs,))] * 2
        + [dma((2,))],
        compiler_params=pltpu.CompilerParams(
            collective_id=0, has_side_effects=True, vmem_limit_bytes=58 * 1024 * 1024
        ),
        cost_estimate=pl.CostEstimate(
            flops=10**11, bytes_accessed=2 * half * aux * depth, transcendentals=0
        ),
        name="pair",
    )(three, mask, g_occ, g_virt, occ_mask, virt_mask)


def body_pair(three, three_mask, g_occ, g_virt, occ_mask, virt_mask):
    half, aux, depth = three.shape
    peers = lax.axis_size(("blk", "sub")) - 1
    mask = three_mask.reshape(-1, depth // BS)
    chi = pair_call(three, mask, g_occ, g_virt, occ_mask, virt_mask, peers)
    return chi.reshape(aux, 3, aux)


def body_any(three, three_mask, g_occ, g_virt, occ_mask, virt_mask):
    eff = mask_three(three, three_mask)
    occ = mask_green(lax.all_gather(g_occ, ("blk", "sub"), axis=0, tiled=True), occ_mask)
    virt = mask_green(lax.all_gather(g_virt, ("blk", "sub"), axis=0, tiled=True), virt_mask)
    whole = lax.all_to_all(eff, "ao", split_axis=1, concat_axis=0, tiled=True)
    left = lax.dot_general(
        whole, occ, (((2,), (0,)), ((), ())), preferred_element_type=jnp.float32
    ).astype(jnp.bfloat16)
    right = lax.dot_general(
        virt, left, (((0,), (0,)), ((), ())), preferred_element_type=jnp.float32
    ).astype(jnp.bfloat16)
    right = lax.all_to_all(right, "ao", split_axis=0, concat_axis=1, tiled=True)
    tiles = [
        lax.dot_general(
            right, other, (((0, 2), (0, 2)), ((), ())), preferred_element_type=jnp.float32
        )
        for other in (shift(eff, ("blk", "sub"), 1), eff, shift(eff, ("blk", "sub"), -1))
    ]
    return lax.psum(jnp.stack(tiles, axis=1), "ao")


def solution(mesh):
    placed = (
        P(("parts", "ao"), ("blk", "sub"), None),
        P(("parts", "ao"), ("blk", "sub"), None),
        P(("parts", "blk", "sub"), None),
        P(("parts", "blk", "sub"), None),
        P("parts", None),
        P("parts", None),
    )
    return jax.shard_map(
        body_pair if mesh.shape["ao"] == 2 else body_any,
        mesh=mesh,
        in_specs=placed,
        out_specs=P(("parts", "blk", "sub"), None, None),
        check_vma=False,
    )
```
